32 devices in a mesh: chan: 4 (over y, x), bl: 8 (over z, core).
Axes of the slice: x: 2, y: 2, z: 4, core: 2. Of those that a mesh axis runs over, the one named last changes fastest.
Arguments:
- grid: float32 [64, 128, 256], P('bl'), may hold values from -6 to 6
- tile_list: int32 [4, 512], P('chan', 'bl'), may hold values from 0 to 63, as said below
- owner_map: int32 [64], replicated, may hold values from 0 to 63, as said below
- offsets: int32 [4, 512, 2], P('chan', 'bl'), may hold values from 4 to 60
- positions: float32 [4, 512, 2, 128], P('chan', 'bl'), may hold values from 0 to 64
- observed: float32 [4, 512, 2, 128], P('chan', 'bl'), may hold values from -6 to 6
- weights: float32 [4, 512, 128], P('chan', 'bl'), may hold values from 0.1 to 1
Outputs:
- new_grid: float32 [64, 128, 256], P('bl', 'chan')
- residual: float32 [4, 512, 2, 128], P('chan', 'bl')
The draws below stay inside these ranges and needn't reach their ends.
Inputs may be any that keep to these rules, and one draw needn't show every extreme that they name: A permutation: tile t lies on index owner_map[t] // 8 of bl, at place owner_map[t] % 8 there. `tile_list`: of the 64 blocks held by one device (one channel group, one index of bl), at most 16 name tiles of any one owner; in every channel group some owner receives exactly 16 blocks from every device of that group.
All inputs are finite; a program needn't handle non-finite values.
Results may differ from the reference program's by a relative error of at most 0.008.
Values sent between devices are 32-bit elements; how exact they have to be, the bound alone decides.
A program may use at most 128 MiB of HBM per device.

```python
import math
import jax
import jax.numpy as jnp
from jax import lax

TILE = 128
VIS = 128
BLK_DEV = 64
TILE_DEV = 8
GROUPS = 4
BLOCKS = 512
TILES = 64
SPAN = 64


def slot_table(key):
    return jax.random.permutation(jax.random.fold_in(key, 7), TILES).astype(jnp.int32)


def draw_owner_map(key, part):
    return slot_table(key)


def draw_tile_list(key, part):
    slots = slot_table(key)
    tile_of_slot = jnp.argsort(slots, stable=True).astype(jnp.int32)
    owners = BLOCKS // BLK_DEV
    capacity = 2 * (BLK_DEV // owners)
    route_key = jax.random.fold_in(key, 11)

    def one_device(group_id, member_id):
        group_key = jax.random.fold_in(route_key, group_id)
        hot_owner = jax.random.randint(group_key, (), 0, owners)
        device_key = jax.random.fold_in(group_key, member_id + 1000)
        key_list = jax.random.split(device_key, 4)
        order = jax.random.permutation(key_list[0], owners - 1).astype(jnp.int32)
        others = order + (order >= hot_owner).astype(jnp.int32)
        pairs = others[1:].reshape(owners // 2 - 1, 2)
        splits = jax.random.randint(key_list[1], (owners // 2 - 1,), 0, capacity + 1)
        counts = jnp.zeros((owners,), jnp.int32).at[hot_owner].set(capacity)
        counts = counts.at[pairs[:, 0]].set(splits).at[pairs[:, 1]].set(capacity - splits)
        bounds = jnp.cumsum(counts)
        places = jnp.arange(BLK_DEV, dtype=jnp.int32)
        owner_seq = jnp.sum((places[:, None] >= bounds[None, :]).astype(jnp.int32), axis=1)
        owner_seq = jax.random.permutation(key_list[2], owner_seq)
        local_slot = jax.random.randint(key_list[3], (BLK_DEV,), 0, TILE_DEV)
        return tile_of_slot[owner_seq * TILE_DEV + local_slot]

    def one_group(group_id):
        return jax.vmap(lambda member_id: one_device(group_id, member_id))(jnp.arange(owners))
    table = jax.vmap(one_group)(jnp.arange(GROUPS))
    return table.reshape(GROUPS, BLOCKS).astype(jnp.int32)


def place_ends(result, rng, least, top_value):
    place = [jax.random.randint(jax.random.fold_in(rng, axis), (), 0, length) for axis, length in enumerate(result.shape)]
    widest = result.shape.index(max(result.shape))
    next_to = place[:widest] + [(place[widest] + 1) % result.shape[widest]] + place[widest + 1:]
    return result.at[tuple(place)].set(least).at[tuple(next_to)].set(top_value)


def level_of(own_key, extent, cuts, smallest, largest):
    level = 1.0
    for position, parts in cuts:
        heights = jax.random.uniform(jax.random.fold_in(jax.random.fold_in(own_key, 6), position), (parts,), jnp.float32, smallest / len(cuts), largest / len(cuts))
        level = level * jnp.repeat(jnp.exp(heights), extent[position] // parts).reshape((-1,) + (1,) * (len(extent) - 1 - position))
    return level


def centred(rng, shape, deviation, limit, cuts=(), held_as=jnp.bfloat16):
    factor_of = level_of(rng, shape, cuts, -0.22, 0.18) if cuts else 1.0
    drawn = jax.random.normal(rng, shape, jnp.float32) * deviation * factor_of
    return jnp.minimum(jnp.maximum(drawn, -limit), limit).astype(held_as)


def setup_inputs(seed: int = 0) -> dict:
    seeds = jax.random.split(jax.random.key(seed), 8)
    return {
        "grid": centred(seeds[0], (TILES, TILE, 2 * TILE), 1.0, 6.0, ((0, 8),), jnp.float32),
        "tile_list": draw_tile_list(jax.random.fold_in(seeds[7], 71), 0),
        "owner_map": draw_owner_map(jax.random.fold_in(seeds[7], 71), 0),
        "offsets": place_ends(jax.random.randint(seeds[3], (GROUPS, BLOCKS, 2), 4, SPAN - 3), jax.random.fold_in(seeds[3], 1), 4, (SPAN - 3) - 1).astype(jnp.int32),
        "positions": jnp.clip(64.0 * jax.random.uniform(seeds[4], (GROUPS, BLOCKS, 2, VIS), jnp.float32) ** level_of(seeds[4], (GROUPS, BLOCKS, 2, VIS), ((0, 4), (1, 8)), -0.2, 0.2), 0.0, 64.0),
        "observed": centred(seeds[5], (GROUPS, BLOCKS, 2, VIS), 1.0, 6.0, ((0, 4), (1, 8)), jnp.float32),
        "weights": jnp.clip(jnp.exp(math.log(1.0) - 2.3025851 * jax.random.uniform(seeds[6], (GROUPS, BLOCKS, VIS), jnp.float32) ** level_of(seeds[6], (GROUPS, BLOCKS, VIS), ((0, 4), (1, 8)), -0.2, 0.2)), 0.1, 1.0),
    }


kernel_beta = 18.4
half_support = 4.0
step_length = 1.0
ridge_weight = 0.5

def spheroid(offset):
    scaled = offset / half_support
    inside = scaled * scaled < 1.0
    root_term = jnp.sqrt(jnp.maximum(1.0 - scaled * scaled, 0.0))
    return jnp.where(inside, jnp.exp(kernel_beta * (root_term - 1.0)), 0.0)

def reference(grid, tile_list, owner_map, offsets, positions, observed, weights):
    tile_width = grid.shape[1]
    grid_low = lax.optimization_barrier(grid.astype(jnp.bfloat16)).astype(jnp.float32)
    tap_offsets = jnp.arange(8, dtype=jnp.int32)

    def one_group(gradient, block_item):
        tile_ids, shift, fraction, observed_now, weight_now = block_item
        slot_index = owner_map[tile_ids].astype(jnp.int32)
        coords = shift.astype(jnp.float32)[..., None] + fraction
        first_cell = jnp.floor(coords).astype(jnp.int32) - 3
        cell_taps = first_cell[..., None] + tap_offsets
        kernel_taps = spheroid(cell_taps.astype(jnp.float32) - coords[..., None]).astype(jnp.bfloat16)
        kernel_taps = lax.optimization_barrier(kernel_taps).astype(jnp.float32)
        kernel_u = kernel_taps[:, 0]
        kernel_v = kernel_taps[:, 1]
        slot_grid = slot_index[:, None, None, None]
        u_rows = cell_taps[:, 0][:, :, :, None]
        v_cols = cell_taps[:, 1][:, :, None, :]
        patch_real = grid_low[slot_grid, u_rows, v_cols]
        patch_imag = grid_low[slot_grid, u_rows, v_cols + tile_width]
        weight_taps = kernel_u[..., :, None] * kernel_v[..., None, :]
        model_real = lax.optimization_barrier(jnp.sum(weight_taps * patch_real, axis=(2, 3)))
        model_imag = lax.optimization_barrier(jnp.sum(weight_taps * patch_imag, axis=(2, 3)))
        residual_now = weight_now[:, None, :] * (jnp.stack([model_real, model_imag], axis=1) - observed_now)
        spread_real = lax.optimization_barrier((residual_now[:, 0, :, None] * kernel_v).astype(jnp.bfloat16)).astype(jnp.float32)
        spread_imag = lax.optimization_barrier((residual_now[:, 1, :, None] * kernel_v).astype(jnp.bfloat16)).astype(jnp.float32)
        update_real = kernel_u[..., :, None] * spread_real[..., None, :]
        update_imag = kernel_u[..., :, None] * spread_imag[..., None, :]
        gradient = gradient.at[slot_grid, u_rows, v_cols].add(update_real)
        gradient = gradient.at[slot_grid, u_rows, v_cols + tile_width].add(update_imag)
        return (gradient, residual_now)
    start_grad = jnp.zeros(grid.shape, jnp.float32)
    gradient, residual = lax.scan(one_group, start_grad, (tile_list, offsets, positions, observed, weights))
    new_grid = grid - step_length * (gradient + ridge_weight * grid)
    return (new_grid, residual)
```

```python
import functools
import math

import jax
import jax.numpy as jnp
from jax import lax
from jax.experimental import pallas as pl
from jax.experimental.pallas import tpu as pltpu
from jax.sharding import PartitionSpec as P

kernel_beta = 18.4
half_support = 4.0
step_length = 1.0
ridge_weight = 0.5
exponent_scale = kernel_beta / math.log(2.0)
MESH = pl.DeviceIdType.MESH
VMEM = pl.BlockSpec(memory_space=pltpu.VMEM)
SMEM = pl.BlockSpec(memory_space=pltpu.SMEM)
ANY = pl.BlockSpec(memory_space=pl.ANY)


def params(**kw):
    return pltpu.CompilerParams(vmem_limit_bytes=24 * 2**20, **kw)


def label_row(cap):
    return -(-5 * cap // 8) * 8


def pack_kernel(cap, tile_dev, tiles, owners, offs, pos, obs, wts, out, place, count):
    blocks = wts.shape[0]
    lab_row = label_row(cap)
    out[...] = jnp.zeros_like(out)
    for o in range(out.shape[0]):
        count[o] = 0
    lane = lax.broadcasted_iota(jnp.int32, (1, out.shape[2]), 1)

    def body(b, carry):
        slot = owners[tiles[0, b]]
        o = lax.div(slot, tile_dev)
        local = lax.rem(slot, tile_dev).astype(jnp.float32)
        r = count[o]
        count[o] = r + 1
        place[b] = o * (2 * cap) + r
        out[o, pl.ds(r, 1), :] = obs[pl.ds(2 * b, 1), :]
        out[o, pl.ds(r + cap, 1), :] = obs[pl.ds(2 * b + 1, 1), :]
        out[o, pl.ds(r + 2 * cap, 1), :] = wts[pl.ds(b, 1), :]
        u_shift = offs[2 * b].astype(jnp.float32)
        v_shift = offs[2 * b + 1].astype(jnp.float32)
        out[o, pl.ds(r + 3 * cap, 1), :] = u_shift + pos[pl.ds(2 * b, 1), :]
        out[o, pl.ds(r + 4 * cap, 1), :] = v_shift + pos[pl.ds(2 * b + 1, 1), :]
        old = out[o, pl.ds(lab_row, 1), :]
        out[o, pl.ds(lab_row, 1), :] = jnp.where(lane == r, local, old)
        return carry

    lax.fori_loop(0, blocks, body, 0, unroll=4)


def exchange_kernel(n, out, grid, came, tiles_t, send_sem, recv_sem, own_sem):
    me = lax.axis_index("bl")
    barrier = pltpu.get_barrier_semaphore()
    for d in range(1, n):
        pl.semaphore_signal(barrier, inc=1, device_id={"bl": lax.rem(me + d, n)}, device_id_type=MESH)
    pl.semaphore_wait(barrier, n - 1)
    copies = []
    for d in range(1, n):
        peer = lax.rem(me + d, n)
        copy = pltpu.make_async_remote_copy(
            src_ref=out.at[peer],
            dst_ref=came.at[me],
            send_sem=send_sem.at[d],
            recv_sem=recv_sem.at[d],
            device_id={"bl": peer},
            device_id_type=MESH,
        )
        copy.start()
        copies.append(copy)
    own = pltpu.make_async_copy(out.at[me], came.at[me], own_sem)
    own.start()
    for t in range(grid.shape[0]):
        tiles_t[t] = grid[t].T.astype(jnp.bfloat16)
    own.wait()
    for copy in copies:
        copy.wait()


def spheroid(cells, coord):
    d = cells - coord * (1.0 / half_support)
    y = 1.0 - d * d
    ym = jnp.maximum(y, 1e-30)
    z = ym * lax.rsqrt(ym) * exponent_scale - exponent_scale
    return jnp.where(y > 0.0, jnp.exp2(z), 0.0)


def compute_kernel(cap, group, labels, came, tiles_t, gradient, residual):
    width = tiles_t.shape[2]
    vis = came.shape[2]
    gradient[...] = jnp.zeros_like(gradient)
    per = cap // group

    def body(i, carry):
        s = lax.div(i, per)
        k0 = lax.rem(i, per) * group
        cells = lax.broadcasted_iota(jnp.int32, (width, vis), 0).astype(jnp.float32) * (
            1.0 / half_support
        )
        contribs = []
        for g in range(group):
            k = k0 + g
            label = labels[s * cap + k]
            rows = [came[s, pl.ds(k + c * cap, 1), :] for c in range(5)]
            ku = spheroid(cells, rows[3]).astype(jnp.bfloat16)
            kv = spheroid(cells, rows[4]).astype(jnp.bfloat16).astype(jnp.float32)
            proj = jnp.dot(tiles_t[label], ku, preferred_element_type=jnp.float32)
            model_re = jnp.sum(proj[:width] * kv, axis=0, keepdims=True)
            model_im = jnp.sum(proj[width:] * kv, axis=0, keepdims=True)
            res_re = rows[2] * (model_re - rows[0])
            res_im = rows[2] * (model_im - rows[1])
            residual[s, pl.ds(k, 1), :] = res_re
            residual[s, pl.ds(k + cap, 1), :] = res_im
            spread = jnp.concatenate(
                [(res_re * kv).astype(jnp.bfloat16), (res_im * kv).astype(jnp.bfloat16)], axis=0
            )
            contribs.append(
                lax.dot_general(
                    ku, spread, (((1,), (1,)), ((), ())), preferred_element_type=jnp.float32
                )
            )
        for g in range(group):
            label = labels[s * cap + k0 + g]
            gradient[label] = gradient[label] + contribs[g]
        return carry

    lax.fori_loop(0, came.shape[0] * per, body, 0)


def finish_kernel(
    n, m, cap, place, residual, gradient, grid, new_grid, res_out,
    back, part, own, send_sem, recv_sem, gsend_sem, grecv_sem, own_sem, mine_sem,
):
    me = lax.axis_index("bl")
    ch = lax.axis_index("chan")
    share = new_grid.shape[1]
    barrier = pltpu.get_barrier_semaphore()
    for d in range(1, m):
        pl.semaphore_signal(barrier, inc=1, device_id={"chan": lax.rem(ch + d, m)}, device_id_type=MESH)
    for d in range(1, n):
        pl.semaphore_signal(barrier, inc=1, device_id={"bl": lax.rem(me + d, n)}, device_id_type=MESH)
    pl.semaphore_wait(barrier, n - 1 + m - 1)
    sums = []
    for d in range(1, m):
        peer = lax.rem(ch + d, m)
        copy = pltpu.make_async_remote_copy(
            src_ref=gradient.at[:, pl.ds(pl.multiple_of(peer * share, share), share), :],
            dst_ref=part.at[d - 1],
            send_sem=gsend_sem.at[d],
            recv_sem=grecv_sem.at[d],
            device_id={"chan": peer},
            device_id_type=MESH,
        )
        copy.start()
        sums.append(copy)
    copies = []
    for d in range(1, n):
        peer = lax.rem(me + d, n)
        copy = pltpu.make_async_remote_copy(
            src_ref=residual.at[peer],
            dst_ref=back.at[pl.ds(pl.multiple_of(me * (2 * cap), 2 * cap), 2 * cap), :],
            send_sem=send_sem.at[d],
            recv_sem=recv_sem.at[d],
            device_id={"bl": peer},
            device_id_type=MESH,
        )
        copy.start()
        copies.append(copy)
    mine = pltpu.make_async_copy(
        residual.at[me], back.at[pl.ds(pl.multiple_of(me * (2 * cap), 2 * cap), 2 * cap), :], mine_sem
    )
    mine.start()
    first = pl.multiple_of(ch * share, share)
    held = pltpu.make_async_copy(grid.at[:, pl.ds(first, share), :], own, own_sem)
    held.start()
    mine.wait()
    for copy in copies:
        copy.wait()

    def unpack(b, carry):
        row = place[b]
        res_out[pl.ds(2 * b, 1), :] = back[pl.ds(row, 1), :]
        res_out[pl.ds(2 * b + 1, 1), :] = back[pl.ds(row + cap, 1), :]
        return carry

    lax.fori_loop(0, res_out.shape[0] // 2, unpack, 0, unroll=4)
    held.wait()
    total = gradient[:, pl.ds(first, share), :]
    for d, copy in enumerate(sums):
        copy.wait()
        total = total + part[d]
    base = own[...]
    new_grid[...] = base - step_length * (total + ridge_weight * base)


def shards(grid, tile_list, owner_map, offsets, positions, observed, weights):
    n = lax.axis_size("bl")
    m = lax.axis_size("chan")
    tile_dev, width, wide = grid.shape
    blocks, vis = tile_list.shape[1], positions.shape[3]
    cap = 2 * blocks // n
    lab_row = label_row(cap)
    f32 = jnp.float32
    out, place = pl.pallas_call(
        functools.partial(pack_kernel, cap, tile_dev),
        out_shape=(
            jax.ShapeDtypeStruct((n, lab_row + 8, vis), f32),
            jax.ShapeDtypeStruct((blocks,), jnp.int32),
        ),
        in_specs=[SMEM, SMEM, SMEM, VMEM, VMEM, VMEM],
        out_specs=(VMEM, SMEM),
        scratch_shapes=[pltpu.SMEM((n,), jnp.int32)],
        compiler_params=params(),
    )(
        tile_list,
        owner_map,
        offsets.reshape(2 * blocks),
        positions.reshape(2 * blocks, vis),
        observed.reshape(2 * blocks, vis),
        weights.reshape(blocks, vis),
    )
    dma = pltpu.SemaphoreType.DMA
    came, tiles_t = pl.pallas_call(
        functools.partial(exchange_kernel, n),
        out_shape=(
            jax.ShapeDtypeStruct(out.shape, f32),
            jax.ShapeDtypeStruct((tile_dev, wide, width), jnp.bfloat16),
        ),
        in_specs=[VMEM, VMEM],
        out_specs=(VMEM, VMEM),
        scratch_shapes=[dma((n,)), dma((n,)), dma],
        compiler_params=params(collective_id=0, has_side_effects=True),
    )(out, grid)
    labels = came[:, lab_row, :cap].astype(jnp.int32).reshape(n * cap)
    gradient, residual = pl.pallas_call(
        functools.partial(compute_kernel, cap, math.gcd(cap, 4)),
        out_shape=(
            jax.ShapeDtypeStruct(grid.shape, f32),
            jax.ShapeDtypeStruct((n, 2 * cap, vis), f32),
        ),
        in_specs=[SMEM, VMEM, VMEM],
        out_specs=(VMEM, VMEM),
        compiler_params=params(),
    )(labels, came, tiles_t)
    share = width // m
    new_grid, res_out = pl.pallas_call(
        functools.partial(finish_kernel, n, m, cap),
        out_shape=(
            jax.ShapeDtypeStruct((tile_dev, share, wide), f32),
            jax.ShapeDtypeStruct((2 * blocks, vis), f32),
        ),
        in_specs=[SMEM, VMEM, VMEM, ANY],
        out_specs=(VMEM, VMEM),
        scratch_shapes=[
            pltpu.VMEM((n * 2 * cap, vis), f32),
            pltpu.VMEM((m - 1, tile_dev, share, wide), f32),
            pltpu.VMEM((tile_dev, share, wide), f32),
            dma((n,)), dma((n,)), dma((m,)), dma((m,)), dma, dma,
        ],
        compiler_params=params(collective_id=1, has_side_effects=True),
    )(place, residual, gradient, grid)
    return (new_grid, res_out.reshape(1, blocks, 2, vis))


def solution(mesh):
    in_specs = (
        P("bl", None, None),
        P("chan", "bl"),
        P(),
        P("chan", "bl", None),
        P("chan", "bl", None, None),
        P("chan", "bl", None, None),
        P("chan", "bl", None),
    )
    out_specs = (P("bl", "chan", None), P("chan", "bl", None, None))
    return jax.shard_map(shards, mesh=mesh, in_specs=in_specs, out_specs=out_specs, check_vma=False)
```

```python
import functools
import math

import jax
import jax.numpy as jnp
from jax import lax
from jax.experimental import pallas as pl
from jax.experimental.pallas import tpu as pltpu
from jax.sharding import PartitionSpec as P

kernel_beta = 18.4
half_support = 4.0
step_length = 1.0
ridge_weight = 0.5
exponent_scale = kernel_beta / math.log(2.0)
MESH = pl.DeviceIdType.MESH
VMEM = pl.BlockSpec(memory_space=pltpu.VMEM)
SMEM = pl.BlockSpec(memory_space=pltpu.SMEM)
ANY = pl.BlockSpec(memory_space=pltpu.HBM)


def params(limit=24, **kw):
    return pltpu.CompilerParams(vmem_limit_bytes=limit * 2**20, **kw)


def pad_rows(cap):
    return -(-5 * cap // 8) * 8


def pack_kernel(
    cap, tile_dev, tiles, owners, offs, pos_in, obs_in, wts_in, out, labels, place,
    count, pos, obs, wts, sems,
):
    loads = [
        pltpu.make_async_copy(src, dst, sems.at[i])
        for i, (src, dst) in enumerate(((pos_in, pos), (obs_in, obs), (wts_in, wts)))
    ]
    for load in loads:
        load.start()
    blocks = wts.shape[0]
    out[...] = jnp.zeros_like(out)
    labels[...] = jnp.zeros_like(labels)
    for o in range(out.shape[0]):
        count[o] = 0
    lane = lax.broadcasted_iota(jnp.int32, (1, out.shape[2]), 1)
    for load in loads:
        load.wait()

    def body(b, carry):
        slot = owners[tiles[0, b]]
        o = lax.div(slot, tile_dev)
        local = lax.rem(slot, tile_dev)
        r = count[o]
        count[o] = r + 1
        place[b] = o * (2 * cap) + r
        out[o, pl.ds(r, 1), :] = obs[pl.ds(2 * b, 1), :]
        out[o, pl.ds(r + cap, 1), :] = obs[pl.ds(2 * b + 1, 1), :]
        out[o, pl.ds(r + 2 * cap, 1), :] = wts[pl.ds(b, 1), :]
        u_shift = offs[0, b].astype(jnp.float32)
        v_shift = offs[1, b].astype(jnp.float32)
        out[o, pl.ds(r + 3 * cap, 1), :] = u_shift + pos[pl.ds(2 * b, 1), :]
        out[o, pl.ds(r + 4 * cap, 1), :] = v_shift + pos[pl.ds(2 * b + 1, 1), :]
        old = labels[o, pl.ds(0, 1), :]
        labels[o, pl.ds(0, 1), :] = jnp.where(lane == r, local, old)
        return carry

    lax.fori_loop(0, blocks, body, 0, unroll=4)


def spheroid(cells, coord):
    d = cells - coord * (1.0 / half_support)
    y = 1.0 - d * d
    ym = jnp.maximum(y, 1e-30)
    z = ym * lax.rsqrt(ym) * exponent_scale - exponent_scale
    return jnp.where(y > 0.0, jnp.exp2(z), 0.0)


def partner(me, d, n):
    peer, bit = me, 1
    while bit < n:
        has = lax.rem(lax.div(d, bit), 2) if not isinstance(d, int) else (d // bit) % 2
        peer = peer + has * bit * (1 - 2 * lax.rem(lax.div(me, bit), 2))
        bit *= 2
    return peer


def degrid_kernel(
    n, cap, group, out, labels, grid_in, came_lab, ku_all, spread_all, residual,
    grid, tiles_t, came, lab_s, send_sem, recv_sem, lsend_sem, lrecv_sem, grid_sem, own_sem, smem_sem,
):
    load = pltpu.make_async_copy(grid_in, grid, grid_sem)
    load.start()
    me = lax.axis_index("bl")
    barrier = pltpu.get_barrier_semaphore()
    for d in range(1, n):
        pl.semaphore_signal(barrier, inc=1, device_id={"bl": partner(me, d, n)}, device_id_type=MESH)
    own_lab = pltpu.make_async_copy(labels.at[me], came_lab.at[me], own_sem.at[0])
    own_lab.start()
    own = pltpu.make_async_copy(out.at[me], came.at[me], own_sem.at[1])
    own.start()
    pl.semaphore_wait(barrier, n - 1)

    def label_copy(d):
        peer = partner(me, d, n)
        return pltpu.make_async_remote_copy(
            src_ref=labels.at[peer],
            dst_ref=came_lab.at[me],
            send_sem=lsend_sem.at[d],
            recv_sem=lrecv_sem.at[d],
            device_id={"bl": peer},
            device_id_type=MESH,
        )

    def data_copy(d):
        peer = partner(me, d, n)
        return pltpu.make_async_remote_copy(
            src_ref=out.at[peer],
            dst_ref=came.at[me],
            send_sem=send_sem.at[d],
            recv_sem=recv_sem.at[d],
            device_id={"bl": peer},
            device_id_type=MESH,
        )

    for d in range(1, n):
        label_copy(d).start()
    for d in range(1, n):
        data_copy(d).start()
    load.wait()
    for t in range(grid.shape[0]):
        tiles_t[t] = grid[t].T.astype(jnp.bfloat16)
    own_lab.wait()
    for d in range(1, n):
        label_copy(d).wait()
    to_smem = pltpu.make_async_copy(came_lab, lab_s, smem_sem)
    to_smem.start()
    to_smem.wait()
    width = tiles_t.shape[2]
    vis = came.shape[2]

    def chunk(s):
        def body(i, carry):
            k0 = i * group
            cells = lax.broadcasted_iota(jnp.int32, (width, vis), 0).astype(jnp.float32) * (
                1.0 / half_support
            )
            for g in range(group):
                k = k0 + g
                label = lab_s[s, 0, k]
                rows = [came[s, pl.ds(k + c * cap, 1), :] for c in range(5)]
                ku = spheroid(cells, rows[3]).astype(jnp.bfloat16)
                kv = spheroid(cells, rows[4]).astype(jnp.bfloat16).astype(jnp.float32)
                proj = jnp.dot(tiles_t[label], ku, preferred_element_type=jnp.float32)
                model_re = jnp.sum(proj[:width] * kv, axis=0, keepdims=True)
                model_im = jnp.sum(proj[width:] * kv, axis=0, keepdims=True)
                res_re = rows[2] * (model_re - rows[0])
                res_im = rows[2] * (model_im - rows[1])
                residual[s, pl.ds(k, 1), :] = res_re
                residual[s, pl.ds(k + cap, 1), :] = res_im
                at = s * cap + k
                ku_all[at] = ku
                spread_all[at, :width, :] = (res_re * kv).astype(jnp.bfloat16)
                spread_all[at, width:, :] = (res_im * kv).astype(jnp.bfloat16)
            return carry

        lax.fori_loop(0, cap // group, body, 0)

    own.wait()
    chunk(me)

    def arrived(d, carry):
        data_copy(d).wait_recv()
        chunk(partner(me, d, n))
        return carry

    lax.fori_loop(1, n, arrived, 0)
    for d in range(1, n):
        data_copy(d).wait_send()


def gradient_kernel(cap, group, labels, ku_all, spread_all, gradient):
    gradient[...] = jnp.zeros_like(gradient)
    per = cap // group

    def body(i, carry):
        s = lax.div(i, per)
        k0 = lax.rem(i, per) * group
        contribs = [
            lax.dot_general(
                ku_all[i * group + g],
                spread_all[i * group + g],
                (((1,), (1,)), ((), ())),
                preferred_element_type=jnp.float32,
            )
            for g in range(group)
        ]
        for g in range(group):
            label = labels[s, 0, k0 + g]
            gradient[label] = gradient[label] + contribs[g]
        return carry

    lax.fori_loop(0, labels.shape[0] * per, body, 0)


def finish_kernel(
    n, m, cap, place, residual, gradient, grid, new_grid, res_out,
    back, part, own, send_sem, recv_sem, gsend_sem, grecv_sem, own_sem, mine_sem,
):
    me = lax.axis_index("bl")
    ch = lax.axis_index("chan")
    share = new_grid.shape[1]
    barrier = pltpu.get_barrier_semaphore()
    for d in range(1, m):
        pl.semaphore_signal(barrier, inc=1, device_id={"chan": lax.rem(ch + d, m)}, device_id_type=MESH)
    for d in range(1, n):
        pl.semaphore_signal(barrier, inc=1, device_id={"bl": lax.rem(me + d, n)}, device_id_type=MESH)
    pl.semaphore_wait(barrier, n - 1 + m - 1)
    sums = []
    for d in range(1, m):
        peer = lax.rem(ch + d, m)
        copy = pltpu.make_async_remote_copy(
            src_ref=gradient.at[:, pl.ds(pl.multiple_of(peer * share, share), share), :],
            dst_ref=part.at[d - 1],
            send_sem=gsend_sem.at[d],
            recv_sem=grecv_sem.at[d],
            device_id={"chan": peer},
            device_id_type=MESH,
        )
        copy.start()
        sums.append(copy)
    copies = []
    for d in range(1, n):
        peer = lax.rem(me + d, n)
        copy = pltpu.make_async_remote_copy(
            src_ref=residual.at[peer],
            dst_ref=back.at[pl.ds(pl.multiple_of(me * (2 * cap), 2 * cap), 2 * cap), :],
            send_sem=send_sem.at[d],
            recv_sem=recv_sem.at[d],
            device_id={"bl": peer},
            device_id_type=MESH,
        )
        copy.start()
        copies.append(copy)
    mine = pltpu.make_async_copy(
        residual.at[me], back.at[pl.ds(pl.multiple_of(me * (2 * cap), 2 * cap), 2 * cap), :], mine_sem
    )
    mine.start()
    first = pl.multiple_of(ch * share, share)
    held = pltpu.make_async_copy(grid.at[:, pl.ds(first, share), :], own, own_sem)
    held.start()
    mine.wait()
    for copy in copies:
        copy.wait()

    def unpack(b, carry):
        row = place[b]
        res_out[pl.ds(2 * b, 1), :] = back[pl.ds(row, 1), :]
        res_out[pl.ds(2 * b + 1, 1), :] = back[pl.ds(row + cap, 1), :]
        return carry

    lax.fori_loop(0, res_out.shape[0] // 2, unpack, 0, unroll=4)
    held.wait()
    total = gradient[:, pl.ds(first, share), :]
    for d, copy in enumerate(sums):
        copy.wait()
        total = total + part[d]
    base = own[...]
    new_grid[...] = base - step_length * (total + ridge_weight * base)


def shards(grid, tile_list, owner_map, offsets, positions, observed, weights):
    n = lax.axis_size("bl")
    m = lax.axis_size("chan")
    tile_dev, width, wide = grid.shape
    blocks, vis = tile_list.shape[1], positions.shape[3]
    cap = 2 * blocks // n
    f32 = jnp.float32
    dma = pltpu.SemaphoreType.DMA
    out, labels, place = pl.pallas_call(
        functools.partial(pack_kernel, cap, tile_dev),
        out_shape=(
            jax.ShapeDtypeStruct((n, pad_rows(cap), vis), f32),
            jax.ShapeDtypeStruct((n, 8, vis), jnp.int32),
            jax.ShapeDtypeStruct((blocks,), jnp.int32),
        ),
        in_specs=[SMEM, SMEM, SMEM, ANY, ANY, ANY],
        out_specs=(VMEM, VMEM, SMEM),
        scratch_shapes=[
            pltpu.SMEM((n,), jnp.int32),
            pltpu.VMEM((2 * blocks, vis), f32),
            pltpu.VMEM((2 * blocks, vis), f32),
            pltpu.VMEM((blocks, vis), f32),
            dma((3,)),
        ],
        compiler_params=params(60),
    )(
        tile_list,
        owner_map,
        jnp.swapaxes(offsets[0], 0, 1),
        positions.reshape(2 * blocks, vis),
        observed.reshape(2 * blocks, vis),
        weights.reshape(blocks, vis),
    )
    group = math.gcd(cap, 4)
    came_lab, ku_all, spread_all, residual = pl.pallas_call(
        functools.partial(degrid_kernel, n, cap, group),
        out_shape=(
            jax.ShapeDtypeStruct((n, 8, vis), jnp.int32),
            jax.ShapeDtypeStruct((n * cap, width, vis), jnp.bfloat16),
            jax.ShapeDtypeStruct((n * cap, wide, vis), jnp.bfloat16),
            jax.ShapeDtypeStruct((n, 2 * cap, vis), f32),
        ),
        in_specs=[VMEM, VMEM, ANY],
        out_specs=(VMEM, VMEM, VMEM, VMEM),
        scratch_shapes=[
            pltpu.VMEM(grid.shape, f32),
            pltpu.VMEM((tile_dev, wide, width), jnp.bfloat16),
            pltpu.VMEM(out.shape, f32),
            pltpu.SMEM((n, 8, vis), jnp.int32),
            dma((n,)), dma((n,)), dma((n,)), dma((n,)), dma, dma((2,)), dma,
        ],
        compiler_params=params(collective_id=0, has_side_effects=True),
    )(out, labels, grid)
    gradient = pl.pallas_call(
        functools.partial(gradient_kernel, cap, group),
        out_shape=jax.ShapeDtypeStruct(grid.shape, f32),
        in_specs=[SMEM, VMEM, VMEM],
        out_specs=VMEM,
        compiler_params=params(),
    )(came_lab, ku_all, spread_all)
    share = width // m
    new_grid, res_out = pl.pallas_call(
        functools.partial(finish_kernel, n, m, cap),
        out_shape=(
            jax.ShapeDtypeStruct((tile_dev, share, wide), f32),
            jax.ShapeDtypeStruct((2 * blocks, vis), f32),
        ),
        in_specs=[SMEM, VMEM, VMEM, ANY],
        out_specs=(VMEM, VMEM),
        scratch_shapes=[
            pltpu.VMEM((n * 2 * cap, vis), f32),
            pltpu.VMEM((m - 1, tile_dev, share, wide), f32),
            pltpu.VMEM((tile_dev, share, wide), f32),
            dma((n,)), dma((n,)), dma((m,)), dma((m,)), dma, dma,
        ],
        compiler_params=params(collective_id=1, has_side_effects=True),
    )(place, residual, gradient, grid)
    return (new_grid, res_out.reshape(1, blocks, 2, vis))


def solution(mesh):
    in_specs = (
        P("bl", None, None),
        P("chan", "bl"),
        P(),
        P("chan", "bl", None),
        P("chan", "bl", None, None),
        P("chan", "bl", None, None),
        P("chan", "bl", None),
    )
    out_specs = (P("bl", "chan", None), P("chan", "bl", None, None))
    return jax.shard_map(shards, mesh=mesh, in_specs=in_specs, out_specs=out_specs, check_vma=False)
```

```python
import functools
import math

import jax
import jax.numpy as jnp
from jax import lax
from jax.experimental import pallas as pl
from jax.experimental.pallas import tpu as pltpu
from jax.sharding import PartitionSpec as P

kernel_beta = 18.4
half_support = 4.0
step_length = 1.0
ridge_weight = 0.5
exponent_scale = kernel_beta / math.log(2.0)
MESH = pl.DeviceIdType.MESH
VMEM = pl.BlockSpec(memory_space=pltpu.VMEM)
SMEM = pl.BlockSpec(memory_space=pltpu.SMEM)
ANY = pl.BlockSpec(memory_space=pltpu.HBM)


def params(limit=24, **kw):
    return pltpu.CompilerParams(vmem_limit_bytes=limit * 2**20, **kw)


def pad_rows(cap):
    return -(-5 * cap // 8) * 8


def pack_kernel(
    cap, tile_dev, tiles, owners, offs, pos_in, obs_in, wts_in, out, labels, place,
    count, pos, obs, wts, sems,
):
    loads = [
        pltpu.make_async_copy(src, dst, sems.at[i])
        for i, (src, dst) in enumerate(((pos_in, pos), (obs_in, obs), (wts_in, wts)))
    ]
    for load in loads:
        load.start()
    blocks = wts.shape[0]
    out[...] = jnp.zeros_like(out)
    labels[...] = jnp.zeros_like(labels)
    for o in range(out.shape[0]):
        count[o] = 0
    lane = lax.broadcasted_iota(jnp.int32, (1, out.shape[2]), 1)
    for load in loads:
        load.wait()

    def body(b, carry):
        slot = owners[tiles[0, b]]
        o = lax.div(slot, tile_dev)
        local = lax.rem(slot, tile_dev)
        r = count[o]
        count[o] = r + 1
        place[b] = o * (2 * cap) + r
        out[o, pl.ds(r, 1), :] = obs[pl.ds(2 * b, 1), :]
        out[o, pl.ds(r + cap, 1), :] = obs[pl.ds(2 * b + 1, 1), :]
        out[o, pl.ds(r + 2 * cap, 1), :] = wts[pl.ds(b, 1), :]
        u_shift = offs[0, b].astype(jnp.float32)
        v_shift = offs[1, b].astype(jnp.float32)
        out[o, pl.ds(r + 3 * cap, 1), :] = u_shift + pos[pl.ds(2 * b, 1), :]
        out[o, pl.ds(r + 4 * cap, 1), :] = v_shift + pos[pl.ds(2 * b + 1, 1), :]
        old = labels[o, pl.ds(0, 1), :]
        labels[o, pl.ds(0, 1), :] = jnp.where(lane == r, local, old)
        return carry

    lax.fori_loop(0, blocks, body, 0, unroll=4)


def spheroid(cells, coord):
    d = cells - coord * (1.0 / half_support)
    y = 1.0 - d * d
    ym = jnp.maximum(y, 1e-30)
    z = ym * lax.rsqrt(ym) * exponent_scale - exponent_scale
    return jnp.where(y > 0.0, jnp.exp2(z), 0.0)


def partner(me, d, n):
    peer, bit = me, 1
    while bit < n:
        has = lax.rem(lax.div(d, bit), 2) if not isinstance(d, int) else (d // bit) % 2
        peer = peer + has * bit * (1 - 2 * lax.rem(lax.div(me, bit), 2))
        bit *= 2
    return peer


def degrid_kernel(
    n, cap, group, out, labels, grid_in, came_lab, ku_all, spread_all, residual,
    grid, tiles_t, came, lab_s, send_sem, recv_sem, lsend_sem, lrecv_sem, grid_sem, own_sem, smem_sem,
):
    load = pltpu.make_async_copy(grid_in, grid, grid_sem)
    load.start()
    me = lax.axis_index("bl")
    barrier = pltpu.get_barrier_semaphore()
    for d in range(1, n):
        pl.semaphore_signal(barrier, inc=1, device_id={"bl": partner(me, d, n)}, device_id_type=MESH)
    own_lab = pltpu.make_async_copy(labels.at[me], came_lab.at[me], own_sem.at[0])
    own_lab.start()
    own = pltpu.make_async_copy(out.at[me], came.at[me], own_sem.at[1])
    own.start()
    pl.semaphore_wait(barrier, n - 1)

    def label_copy(d):
        peer = partner(me, d, n)
        return pltpu.make_async_remote_copy(
            src_ref=labels.at[peer],
            dst_ref=came_lab.at[me],
            send_sem=lsend_sem.at[d],
            recv_sem=lrecv_sem.at[d],
            device_id={"bl": peer},
            device_id_type=MESH,
        )

    def data_copy(d):
        peer = partner(me, d, n)
        return pltpu.make_async_remote_copy(
            src_ref=out.at[peer],
            dst_ref=came.at[me],
            send_sem=send_sem.at[d],
            recv_sem=recv_sem.at[d],
            device_id={"bl": peer},
            device_id_type=MESH,
        )

    for d in range(1, n):
        label_copy(d).start()
    for d in range(1, n):
        data_copy(d).start()
    load.wait()
    for t in range(grid.shape[0]):
        tiles_t[t] = grid[t].T.astype(jnp.bfloat16)
    own_lab.wait()
    for d in range(1, n):
        label_copy(d).wait()
    to_smem = pltpu.make_async_copy(came_lab, lab_s, smem_sem)
    to_smem.start()
    to_smem.wait()
    width = tiles_t.shape[2]
    vis = came.shape[2]

    def chunk(s):
        def body(i, carry):
            k0 = i * group
            cells = lax.broadcasted_iota(jnp.int32, (width, vis), 0).astype(jnp.float32) * (
                1.0 / half_support
            )
            each = range(group)
            rows = [[came[s, pl.ds(k0 + g + c * cap, 1), :] for c in range(5)] for g in each]
            held = [tiles_t[lab_s[s, 0, k0 + g]] for g in each]
            kus = [spheroid(cells, rows[g][3]).astype(jnp.bfloat16) for g in each]
            projs = [jnp.dot(held[g], kus[g], preferred_element_type=jnp.float32) for g in each]
            kvs = [
                spheroid(cells, rows[g][4]).astype(jnp.bfloat16).astype(jnp.float32) for g in each
            ]
            res_re = [
                rows[g][2] * (jnp.sum(projs[g][:width] * kvs[g], axis=0, keepdims=True) - rows[g][0])
                for g in each
            ]
            res_im = [
                rows[g][2] * (jnp.sum(projs[g][width:] * kvs[g], axis=0, keepdims=True) - rows[g][1])
                for g in each
            ]
            for g in each:
                at = s * cap + k0 + g
                residual[s, pl.ds(k0 + g, 1), :] = res_re[g]
                residual[s, pl.ds(k0 + g + cap, 1), :] = res_im[g]
                ku_all[at] = kus[g]
                spread_all[at, :width, :] = (res_re[g] * kvs[g]).astype(jnp.bfloat16)
                spread_all[at, width:, :] = (res_im[g] * kvs[g]).astype(jnp.bfloat16)
            return carry

        lax.fori_loop(0, cap // group, body, 0)

    own.wait()
    chunk(me)

    def arrived(d, carry):
        data_copy(d).wait_recv()
        chunk(partner(me, d, n))
        return carry

    lax.fori_loop(1, n, arrived, 0)
    for d in range(1, n):
        data_copy(d).wait_send()


def gradient_kernel(cap, group, labels, ku_all, spread_all, gradient):
    gradient[...] = jnp.zeros_like(gradient)
    per = cap // group

    def body(i, carry):
        s = lax.div(i, per)
        k0 = lax.rem(i, per) * group
        contribs = [
            lax.dot_general(
                ku_all[i * group + g],
                spread_all[i * group + g],
                (((1,), (1,)), ((), ())),
                preferred_element_type=jnp.float32,
            )
            for g in range(group)
        ]
        for g in range(group):
            label = labels[s, 0, k0 + g]
            gradient[label] = gradient[label] + contribs[g]
        return carry

    lax.fori_loop(0, labels.shape[0] * per, body, 0)


def finish_kernel(
    n, m, cap, place, residual, gradient, grid, new_grid, res_out,
    back, part, own, send_sem, recv_sem, gsend_sem, grecv_sem, own_sem, mine_sem,
):
    me = lax.axis_index("bl")
    ch = lax.axis_index("chan")
    share = new_grid.shape[1]
    barrier = pltpu.get_barrier_semaphore()
    for d in range(1, m):
        pl.semaphore_signal(barrier, inc=1, device_id={"chan": lax.rem(ch + d, m)}, device_id_type=MESH)
    for d in range(1, n):
        pl.semaphore_signal(barrier, inc=1, device_id={"bl": lax.rem(me + d, n)}, device_id_type=MESH)
    pl.semaphore_wait(barrier, n - 1 + m - 1)
    sums = []
    for d in range(1, m):
        peer = lax.rem(ch + d, m)
        copy = pltpu.make_async_remote_copy(
            src_ref=gradient.at[:, pl.ds(pl.multiple_of(peer * share, share), share), :],
            dst_ref=part.at[d - 1],
            send_sem=gsend_sem.at[d],
            recv_sem=grecv_sem.at[d],
            device_id={"chan": peer},
            device_id_type=MESH,
        )
        copy.start()
        sums.append(copy)
    copies = []
    for d in range(1, n):
        peer = lax.rem(me + d, n)
        copy = pltpu.make_async_remote_copy(
            src_ref=residual.at[peer],
            dst_ref=back.at[pl.ds(pl.multiple_of(me * (2 * cap), 2 * cap), 2 * cap), :],
            send_sem=send_sem.at[d],
            recv_sem=recv_sem.at[d],
            device_id={"bl": peer},
            device_id_type=MESH,
        )
        copy.start()
        copies.append(copy)
    mine = pltpu.make_async_copy(
        residual.at[me], back.at[pl.ds(pl.multiple_of(me * (2 * cap), 2 * cap), 2 * cap), :], mine_sem
    )
    mine.start()
    first = pl.multiple_of(ch * share, share)
    held = pltpu.make_async_copy(grid.at[:, pl.ds(first, share), :], own, own_sem)
    held.start()
    mine.wait()
    for copy in copies:
        copy.wait()

    def unpack(b, carry):
        row = place[b]
        res_out[pl.ds(2 * b, 1), :] = back[pl.ds(row, 1), :]
        res_out[pl.ds(2 * b + 1, 1), :] = back[pl.ds(row + cap, 1), :]
        return carry

    lax.fori_loop(0, res_out.shape[0] // 2, unpack, 0, unroll=4)
    held.wait()
    total = gradient[:, pl.ds(first, share), :]
    for d, copy in enumerate(sums):
        copy.wait()
        total = total + part[d]
    base = own[...]
    new_grid[...] = base - step_length * (total + ridge_weight * base)


def shards(grid, tile_list, owner_map, offsets, positions, observed, weights):
    n = lax.axis_size("bl")
    m = lax.axis_size("chan")
    tile_dev, width, wide = grid.shape
    blocks, vis = tile_list.shape[1], positions.shape[3]
    cap = 2 * blocks // n
    f32 = jnp.float32
    dma = pltpu.SemaphoreType.DMA
    out, labels, place = pl.pallas_call(
        functools.partial(pack_kernel, cap, tile_dev),
        out_shape=(
            jax.ShapeDtypeStruct((n, pad_rows(cap), vis), f32),
            jax.ShapeDtypeStruct((n, 8, vis), jnp.int32),
            jax.ShapeDtypeStruct((blocks,), jnp.int32),
        ),
        in_specs=[SMEM, SMEM, SMEM, ANY, ANY, ANY],
        out_specs=(VMEM, VMEM, SMEM),
        scratch_shapes=[
            pltpu.SMEM((n,), jnp.int32),
            pltpu.VMEM((2 * blocks, vis), f32),
            pltpu.VMEM((2 * blocks, vis), f32),
            pltpu.VMEM((blocks, vis), f32),
            dma((3,)),
        ],
        compiler_params=params(60),
    )(
        tile_list,
        owner_map,
        jnp.swapaxes(offsets[0], 0, 1),
        positions.reshape(2 * blocks, vis),
        observed.reshape(2 * blocks, vis),
        weights.reshape(blocks, vis),
    )
    group = math.gcd(cap, 4)
    came_lab, ku_all, spread_all, residual = pl.pallas_call(
        functools.partial(degrid_kernel, n, cap, group),
        out_shape=(
            jax.ShapeDtypeStruct((n, 8, vis), jnp.int32),
            jax.ShapeDtypeStruct((n * cap, width, vis), jnp.bfloat16),
            jax.ShapeDtypeStruct((n * cap, wide, vis), jnp.bfloat16),
            jax.ShapeDtypeStruct((n, 2 * cap, vis), f32),
        ),
        in_specs=[VMEM, VMEM, ANY],
        out_specs=(VMEM, VMEM, VMEM, VMEM),
        scratch_shapes=[
            pltpu.VMEM(grid.shape, f32),
            pltpu.VMEM((tile_dev, wide, width), jnp.bfloat16),
            pltpu.VMEM(out.shape, f32),
            pltpu.SMEM((n, 8, vis), jnp.int32),
            dma((n,)), dma((n,)), dma((n,)), dma((n,)), dma, dma((2,)), dma,
        ],
        compiler_params=params(collective_id=0, has_side_effects=True),
    )(out, labels, grid)
    gradient = pl.pallas_call(
        functools.partial(gradient_kernel, cap, group),
        out_shape=jax.ShapeDtypeStruct(grid.shape, f32),
        in_specs=[SMEM, VMEM, VMEM],
        out_specs=VMEM,
        compiler_params=params(),
    )(came_lab, ku_all, spread_all)
    share = width // m
    new_grid, res_out = pl.pallas_call(
        functools.partial(finish_kernel, n, m, cap),
        out_shape=(
            jax.ShapeDtypeStruct((tile_dev, share, wide), f32),
            jax.ShapeDtypeStruct((2 * blocks, vis), f32),
        ),
        in_specs=[SMEM, VMEM, VMEM, ANY],
        out_specs=(VMEM, VMEM),
        scratch_shapes=[
            pltpu.VMEM((n * 2 * cap, vis), f32),
            pltpu.VMEM((m - 1, tile_dev, share, wide), f32),
            pltpu.VMEM((tile_dev, share, wide), f32),
            dma((n,)), dma((n,)), dma((m,)), dma((m,)), dma, dma,
        ],
        compiler_params=params(collective_id=1, has_side_effects=True),
    )(place, residual, gradient, grid)
    return (new_grid, res_out.reshape(1, blocks, 2, vis))


def solution(mesh):
    in_specs = (
        P("bl", None, None),
        P("chan", "bl"),
        P(),
        P("chan", "bl", None),
        P("chan", "bl", None, None),
        P("chan", "bl", None, None),
        P("chan", "bl", None),
    )
    out_specs = (P("bl", "chan", None), P("chan", "bl", None, None))
    return jax.shard_map(shards, mesh=mesh, in_specs=in_specs, out_specs=out_specs, check_vma=False)
```
